32 devices in a mesh: gx: 4 (over y, x), gy: 2 (over core), gz: 4 (over z).
Axes of the slice: x: 2, y: 2, z: 4, core: 2. Of those that a mesh axis runs over, the one named last changes fastest.
Arguments:
- leaf_multipoles: float32 [32768, 152], P(('gx', 'gy', 'gz')), may hold values from -6 to 6
- upward_ops: float32 [8, 152, 152], replicated, may hold values from -0.15625 to 0.15625
- transfer_ops: float32 [16, 152, 152], replicated, may hold values from -0.15625 to 0.15625
- downward_ops: float32 [8, 152, 152], replicated, may hold values from -0.5 to 0.5
- send_cells: int32 [32, 4, 32], P(('gx', 'gy', 'gz')), may hold values from 0 to 127
- send_count: int32 [32, 4], P(('gx', 'gy', 'gz')), may hold values from 1 to 32, as said below
- list_source: int32 [32, 16, 128], P(('gx', 'gy', 'gz')), may hold values from 0 to 255
- list_target: int32 [32, 16, 128], P(('gx', 'gy', 'gz')), may hold values from 0 to 127, as said below
- list_count: int32 [32, 16], P(('gx', 'gy', 'gz')), may hold values from 32 to 128, as said below
Outputs:
- leaf_locals: float32 [32768, 152], P(('gx', 'gy', 'gz'))
The draws below stay inside these ranges and needn't reach their ends.
Inputs may be any that keep to these rules, and one draw needn't show every extreme that they name: `send_count`: in each row one count equals 32, at a peer drawn from the seed. `list_count`: in each row one count equals 128, at an operator drawn from the seed. `list_target`: for each device and operator the 128 entries are a permutation of the local cells, so the used slots name distinct targets.
All inputs are finite; a program needn't handle non-finite values.
Results may differ from the reference program's by a relative error of at most 0.0003.
Values sent between devices are 32-bit elements; how exact they have to be, the bound alone decides.
A program may use at most 64 MiB of HBM per device.

```python
import jax
import jax.numpy as jnp
from jax import lax

COEFS = 152
CELL_DEV = 128
OPS = 16
SLOTS = 32
LIST_W = 128
LEAVES = 32768
N_GZ = 4
DEVICES = 32


def draw_send_count(key, part):
    key = jax.random.fold_in(key, 11)
    first, second = jax.random.split(key)
    counts = jax.random.randint(first, (DEVICES, N_GZ), 1, SLOTS + 1)
    column = jax.random.randint(second, (DEVICES,), 0, N_GZ)
    full = column[:, None] == jnp.arange(N_GZ)[None, :]
    return jnp.where(full, SLOTS, counts).astype(jnp.int32)


def draw_list_count(key, part):
    key = jax.random.fold_in(key, 23)
    first, second = jax.random.split(key)
    counts = jax.random.randint(first, (DEVICES, OPS), LIST_W // 4, LIST_W + 1)
    column = jax.random.randint(second, (DEVICES,), 0, OPS)
    full = column[:, None] == jnp.arange(OPS)[None, :]
    return jnp.where(full, LIST_W, counts).astype(jnp.int32)


def draw_list_target(key, part):
    key = jax.random.fold_in(key, 37)
    scores = jax.random.randint(key, (DEVICES, OPS, LIST_W), 0, 1048576)
    scores = scores * LIST_W + jnp.arange(LIST_W, dtype=jnp.int32)[None, None, :]
    return jnp.argsort(scores, axis=-1).astype(jnp.int32)


def plant(array, stream_key, smallest, high):
    longest = array.shape.index(max(array.shape))
    spots = []
    for shift in (0, 1):
        where = [jax.random.randint(jax.random.fold_in(stream_key, axis), (), 0, length) for axis, length in enumerate(array.shape)]
        where[longest] = (where[longest] + shift) % array.shape[longest]
        spots.append(tuple(where))
    return array.at[spots[0]].set(smallest).at[spots[1]].set(high)


def shard_levels(key, dims, cuts, low, largest):
    factor_of = 1.0
    for dim, parts in cuts:
        steps = jax.random.uniform(jax.random.fold_in(jax.random.fold_in(key, 6), dim), (parts,), jnp.float32, low / len(cuts), largest / len(cuts))
        factor_of = factor_of * jnp.repeat(jnp.exp(steps), dims[dim] // parts).reshape((-1,) + (1,) * (len(dims) - 1 - dim))
    return factor_of


def noise(stream_key, shape, deviation, most, pieces=(), kind=jnp.bfloat16):
    drawn = deviation * jax.random.normal(stream_key, shape, jnp.float32)
    if pieces:
        drawn = drawn * shard_levels(stream_key, shape, pieces, -0.22, 0.18)
    return jnp.clip(drawn, -most, most).astype(kind)


def setup_inputs(seed: int = 0) -> dict:
    key_of = jax.random.split(jax.random.key(seed), 10)
    leaf_multipoles = noise(key_of[0], (LEAVES, COEFS), 1.0, 6.0, ((0, 32),), jnp.float32)
    upward_ops = noise(key_of[1], (8, COEFS, COEFS), (8 * COEFS) ** -0.5, 0.15625, (), jnp.float32)
    transfer_ops = noise(key_of[2], (OPS, COEFS, COEFS), (8 * COEFS) ** -0.5, 0.15625, (), jnp.float32)
    downward_ops = noise(key_of[3], (8, COEFS, COEFS), COEFS ** -0.5, 0.5, (), jnp.float32)
    send_cells = plant(jax.random.randint(key_of[4], (DEVICES, N_GZ, SLOTS), 0, CELL_DEV), jax.random.fold_in(key_of[4], 1), 0, CELL_DEV - 1).astype(jnp.int32)
    send_count = draw_send_count(jax.random.fold_in(key_of[9], 71), 0)
    list_source = plant(jax.random.randint(key_of[6], (DEVICES, OPS, LIST_W), 0, CELL_DEV + N_GZ * SLOTS), jax.random.fold_in(key_of[6], 1), 0, (CELL_DEV + N_GZ * SLOTS) - 1).astype(jnp.int32)
    list_target = draw_list_target(jax.random.fold_in(key_of[9], 71), 0)
    list_count = draw_list_count(jax.random.fold_in(key_of[9], 71), 0)
    return {"leaf_multipoles": leaf_multipoles, "upward_ops": upward_ops, "transfer_ops": transfer_ops, "downward_ops": downward_ops, "send_cells": send_cells, "send_count": send_count, "list_source": list_source, "list_target": list_target, "list_count": list_count}


def reference(leaf_multipoles, upward_ops, transfer_ops, downward_ops, send_cells, send_count, list_source, list_target, list_count):
    highest = lax.Precision.HIGHEST
    cell_total = CELL_DEV * DEVICES
    cell_multipoles = jnp.einsum("ckp,kpq->cq", leaf_multipoles.reshape(cell_total, 8, COEFS), upward_ops, precision=highest)
    octant_sums = cell_multipoles.reshape(DEVICES, CELL_DEV // 8, 8, COEFS).sum(1)
    top_multipoles = (8.0 / CELL_DEV) ** 0.5 * jnp.einsum("dkp,kpq->dq", octant_sums, upward_ops, precision=highest)
    device_ids = jnp.arange(DEVICES, dtype=jnp.int32)
    mixed_ids = jnp.bitwise_xor(device_ids[:, None], device_ids[None, :])
    op_ids = jnp.arange(OPS, dtype=jnp.int32)
    onehot = ((mixed_ids[None] % OPS == op_ids[:, None, None]) & (mixed_ids[None] >= N_GZ)).astype(jnp.float32)
    grouped_top = jnp.einsum("kij,jp->kip", onehot, top_multipoles, precision=highest)
    top_locals = (32.0 / DEVICES) ** 0.5 * jnp.einsum("kip,kpq->iq", grouped_top, transfer_ops, precision=highest)
    downward_top = jnp.einsum("ip,kpq->ikq", top_locals, downward_ops, precision=highest)
    slot_ids = jnp.arange(SLOTS, dtype=jnp.int32)
    width_ids = jnp.arange(LIST_W, dtype=jnp.int32)
    peer_ids = jnp.arange(N_GZ, dtype=jnp.int32)

    def one_device(device):
        position = device % N_GZ
        sources = (device - position + peer_ids).astype(jnp.int32)
        send_rows = send_cells[sources, position]
        counts = send_count[sources, position]
        picked = cell_multipoles[sources[:, None] * CELL_DEV + send_rows]
        picked = picked * (slot_ids[None] < counts[:, None]).astype(jnp.float32)[..., None]
        own_cells = lax.dynamic_slice_in_dim(cell_multipoles, (device * CELL_DEV).astype(jnp.int32), CELL_DEV, 0)
        table = jnp.concatenate([own_cells, picked.reshape(N_GZ * SLOTS, COEFS)], 0)
        active = (width_ids[None] < list_count[device][:, None]).astype(jnp.float32)
        rows_used = table[list_source[device]] * active[..., None]
        grouped = jnp.zeros((OPS, CELL_DEV, COEFS), jnp.float32).at[op_ids[:, None], list_target[device]].add(rows_used)
        total = jnp.einsum("kcp,kpq->cq", grouped, transfer_ops, precision=highest)
        cell_locals = (total.reshape(CELL_DEV // 8, 8, COEFS) + downward_top[device][None]).reshape(CELL_DEV, COEFS)
        return jnp.einsum("cp,kpq->ckq", cell_locals, downward_ops, precision=highest).reshape(8 * CELL_DEV, COEFS)

    leaf_locals = lax.map(one_device, device_ids)
    return leaf_locals.reshape(LEAVES, COEFS)
```

```python
import functools

import jax
import jax.numpy as jnp
from jax import lax
from jax.experimental import pallas as pl
from jax.experimental.pallas import tpu as pltpu
from jax.sharding import PartitionSpec as P

MESH = pl.DeviceIdType.MESH
F32 = jnp.float32
BF16 = jnp.bfloat16
NT = (((1,), (1,)), ((), ()))
TN = (((0,), (0,)), ((), ()))


def split(value):
    high = value.astype(BF16)
    return high, (value - high.astype(F32)).astype(BF16)


def dot(a, b):
    return jnp.dot(a, b, preferred_element_type=F32)


def dot3(a, b):
    return dot(a[0], b[0]) + dot(a[0], b[1]) + dot(a[1], b[0])


def xor(a, b, size):
    total, bit = 0, 1
    while bit < size:
        total = total + ((a // bit + b // bit) % 2) * bit
        bit *= 2
    return total


def equal(row, length):
    rows = lax.broadcasted_iota(jnp.int32, (length, row.shape[1]), 0)
    return jnp.where(rows == row, 1.0, 0.0).astype(BF16)


def kernel(
    sizes,
    leaf_hbm, up_hbm, transfer_hbm, down_hbm,
    cells_hbm, sends_hbm, source_hbm, target_hbm, counts_hbm,
    out_ref,
    leaf, up, transfer, down,
    cells, sends, source, target, counts,
    up_high, up_low, transfer_high, transfer_low, down_high, down_low,
    choose, outgoing, received, top_row, tops, picked_high, picked_low,
    load_sem, send_sem, recv_sem, top_send_sem, top_recv_sem,
):
    n_gx, n_gy, n_gz = sizes
    devices = n_gx * n_gy * n_gz
    cell_count, _, coefs = leaf.shape
    ops = transfer.shape[0]
    slots = cells.shape[1]
    rows = cell_count + n_gz * slots
    i_gx, i_gy, i_gz = lax.axis_index("gx"), lax.axis_index("gy"), lax.axis_index("gz")

    def peer(x):
        return (
            xor(i_gx, x // (n_gz * n_gy), n_gx),
            xor(i_gy, (x // n_gz) % n_gy, n_gy),
            xor(i_gz, x % n_gz, n_gz),
        )

    def each(low, high, body):
        if devices <= 64:
            for x in range(low, high):
                body(x)
        else:
            lax.fori_loop(low, high, lambda x, c: (body(x), c)[1], 0)

    loads = [
        pltpu.make_async_copy(src, dst, load_sem.at[i])
        for i, (src, dst) in enumerate(
            [
                (source_hbm.at[0], source),
                (target_hbm.at[0], target),
                (counts_hbm, counts),
                (cells_hbm.at[0], cells),
                (sends_hbm, sends),
                (leaf_hbm, leaf),
                (up_hbm, up),
                (transfer_hbm, transfer),
                (down_hbm, down),
            ]
        )
    ]
    for load in loads:
        load.start()

    barrier = pltpu.get_barrier_semaphore()
    each(
        1,
        devices,
        lambda x: pl.semaphore_signal(barrier, inc=1, device_id=peer(x), device_id_type=MESH),
    )

    for load in loads[:5]:
        load.wait()
    lane = lax.broadcasted_iota(jnp.int32, (1, target.shape[1]), 1)
    for k in range(ops):
        used = jnp.where(lane < counts[0:1, k : k + 1], target[k : k + 1, :], -1)
        choose[pl.ds(k * cell_count, cell_count), :] = lax.dot_general(
            equal(used, cell_count),
            equal(source[k : k + 1, :], rows),
            NT,
            preferred_element_type=F32,
        ).astype(BF16)
    lane = lax.broadcasted_iota(jnp.int32, (1, slots), 1)
    wanted = jnp.concatenate(
        [
            jnp.where(lane < sends[0:1, s : s + 1], cells[s : s + 1, :], -1)
            for s in range(n_gz)
        ],
        axis=1,
    )
    pick = equal(wanted, cell_count)

    loads[5].wait()
    loads[6].wait()
    cell = jnp.zeros((cell_count, coefs), F32)
    for k in range(8):
        up_high[k], up_low[k] = split(up[k])
        cell = cell + dot3(split(leaf[:, k, :]), (up_high[k], up_low[k]))
    cell_high, cell_low = split(cell)
    out_rows = lax.dot_general(pick, cell_high, TN, preferred_element_type=F32) + lax.dot_general(
        pick, cell_low, TN, preferred_element_type=F32
    )
    outgoing[...] = out_rows.reshape(n_gz, slots, coefs)
    pl.semaphore_wait(barrier, devices - 1)

    def cell_copy(x):
        to = peer(x)
        return pltpu.make_async_remote_copy(
            src_ref=outgoing.at[to[2]],
            dst_ref=received.at[i_gz],
            send_sem=send_sem.at[x],
            recv_sem=recv_sem.at[x],
            device_id=to,
            device_id_type=MESH,
        )

    cell_copies = [cell_copy(x) for x in range(1, n_gz)]
    for copy in cell_copies:
        copy.start()

    octants = split(cell.reshape(cell_count // 8, 8, coefs).sum(0))
    top = jnp.zeros((8, coefs), F32)
    eight = lax.broadcasted_iota(jnp.int32, (8, coefs), 0)
    for k in range(8):
        top = top + jnp.where(eight == k, dot3(octants, (up_high[k], up_low[k])), 0.0)
    top_row[...] = (8.0 / cell_count) ** 0.5 * top.sum(0, keepdims=True)

    def send_top(x):
        pltpu.make_async_remote_copy(
            src_ref=top_row,
            dst_ref=tops.at[x],
            send_sem=top_send_sem,
            recv_sem=top_recv_sem,
            device_id=peer(x),
            device_id_type=MESH,
        ).start()

    each(n_gz, devices, send_top)

    loads[7].wait()
    for k in range(ops):
        transfer_high[k], transfer_low[k] = split(transfer[k])
    loads[8].wait()
    for k in range(8):
        down_high[k], down_low[k] = split(down[k])
    received[i_gz] = outgoing[i_gz]

    for copy in cell_copies:
        copy.wait_recv()
    got_high, got_low = split(received[...].reshape(n_gz * slots, coefs))
    table_high = jnp.concatenate([cell_high, got_high], axis=0)
    table_low = jnp.concatenate([cell_low, got_low], axis=0)
    for k in range(ops):
        chosen = choose[pl.ds(k * cell_count, cell_count), :]
        picked_high[k, 0:cell_count, :] = dot(chosen, table_high).astype(BF16)
        picked_low[k, 0:cell_count, :] = dot(chosen, table_low).astype(BF16)

    far = tops.at[pl.ds(n_gz, devices - n_gz)]
    pltpu.make_async_copy(far, far, top_recv_sem).wait()
    for k in range(ops):
        extra = jnp.zeros((1, coefs), F32)
        for x in range(k, devices, ops):
            if x >= n_gz:
                extra = extra + tops[x]
        picked_high[k, cell_count : cell_count + 16, :], picked_low[
            k, cell_count : cell_count + 16, :
        ] = split(jnp.broadcast_to(extra, (16, coefs)))
    total = jnp.zeros((cell_count + 16, coefs), F32)
    for k in range(ops):
        total = total + dot3(
            (picked_high[k], picked_low[k]), (transfer_high[k], transfer_low[k])
        )
    coarse = split((32.0 / devices) ** 0.5 * total[cell_count:])
    coarse_down = jnp.zeros((8, coefs), F32)
    for k in range(8):
        coarse_down = coarse_down + jnp.where(
            eight == k, dot3(coarse, (down_high[k], down_low[k]))[0:8], 0.0
        )
    near = total[0:cell_count].reshape(cell_count // 8, 8, coefs)
    local_cells = split((near + coarse_down[None]).reshape(cell_count, coefs))
    for k in range(8):
        out_ref[:, k, :] = dot3(local_cells, (down_high[k], down_low[k]))

    for copy in cell_copies:
        copy.wait_send()
    pltpu.make_async_copy(far, far, top_send_sem).wait()


def local(sizes, leaf_multipoles, upward_ops, transfer_ops, downward_ops, *lists):
    leaves, coefs = leaf_multipoles.shape
    cell_count = leaves // 8
    ops = transfer_ops.shape[0]
    send_cells, send_count, list_source, list_target, list_count = lists
    n_gz, slots = send_cells.shape[1:]
    devices = sizes[0] * sizes[1] * sizes[2]
    rows = cell_count + n_gz * slots
    vmem = pltpu.VMEM
    weights = lambda n: [vmem((n, coefs, coefs), BF16)] * 2
    out = pl.pallas_call(
        functools.partial(kernel, sizes),
        out_shape=jax.ShapeDtypeStruct((cell_count, 8, coefs), F32),
        in_specs=[pl.BlockSpec(memory_space=pl.ANY)] * 9,
        out_specs=pl.BlockSpec(memory_space=pltpu.VMEM),
        scratch_shapes=[
            vmem((cell_count, 8, coefs), F32),
            vmem(upward_ops.shape, F32),
            vmem(transfer_ops.shape, F32),
            vmem(downward_ops.shape, F32),
            vmem(send_cells.shape[1:], jnp.int32),
            vmem(send_count.shape, jnp.int32),
            vmem(list_source.shape[1:], jnp.int32),
            vmem(list_target.shape[1:], jnp.int32),
            vmem(list_count.shape, jnp.int32),
            *weights(8),
            *weights(ops),
            *weights(8),
            vmem((ops * cell_count, rows), BF16),
            vmem((n_gz, slots, coefs), F32),
            vmem((n_gz, slots, coefs), F32),
            vmem((1, coefs), F32),
            vmem((devices, 1, coefs), F32),
            vmem((ops, cell_count + 16, coefs), BF16),
            vmem((ops, cell_count + 16, coefs), BF16),
            pltpu.SemaphoreType.DMA((9,)),
            pltpu.SemaphoreType.DMA((n_gz,)),
            pltpu.SemaphoreType.DMA((n_gz,)),
            pltpu.SemaphoreType.DMA,
            pltpu.SemaphoreType.DMA,
        ],
        compiler_params=pltpu.CompilerParams(
            collective_id=0, has_side_effects=True, vmem_limit_bytes=48 << 20
        ),
        cost_estimate=pl.CostEstimate(
            flops=6 * 2 * 32 * cell_count * coefs * coefs,
            bytes_accessed=8_000_000,
            transcendentals=0,
        ),
    )(leaf_multipoles.reshape(cell_count, 8, coefs), upward_ops, transfer_ops, downward_ops, *lists)
    return out.reshape(leaves, coefs)


def solution(mesh):
    sizes = tuple(mesh.shape[name] for name in ("gx", "gy", "gz"))
    split_all = ("gx", "gy", "gz")
    return jax.shard_map(
        functools.partial(local, sizes),
        mesh=mesh,
        in_specs=(
            P(split_all, None),
            P(),
            P(),
            P(),
            P(split_all, None, None),
            P(split_all, None),
            P(split_all, None, None),
            P(split_all, None, None),
            P(split_all, None),
        ),
        out_specs=P(split_all, None),
        check_vma=False,
    )
```

```python
import functools

import jax
import jax.numpy as jnp
from jax import lax
from jax.experimental import pallas as pl
from jax.experimental.pallas import tpu as pltpu
from jax.sharding import PartitionSpec as P

MESH = pl.DeviceIdType.MESH
F32 = jnp.float32
BF16 = jnp.bfloat16
NT = (((1,), (1,)), ((), ()))
TN = (((0,), (0,)), ((), ()))


def split(value):
    high = value.astype(BF16)
    return high, (value - high.astype(F32)).astype(BF16)


def dot(a, b):
    return jnp.dot(a, b, preferred_element_type=F32)


def dot3(a, b):
    return dot(a[0], b[0]) + dot(a[0], b[1]) + dot(a[1], b[0])


def xor(a, b, size):
    total, bit = 0, 1
    while bit < size:
        total = total + ((a // bit + b // bit) % 2) * bit
        bit *= 2
    return total


def equal(row, length):
    rows = lax.broadcasted_iota(jnp.int32, (length, row.shape[1]), 0)
    return jnp.where(rows == row, 1.0, 0.0).astype(BF16)


def kernel(
    sizes,
    leaf_hbm, up_hbm, transfer_hbm, down_hbm,
    cells_hbm, sends_hbm, source_hbm, target_hbm, counts_hbm,
    out_ref,
    leaf, up, transfer, down,
    cells, sends, source, target, counts,
    leaf_high, leaf_low, transfer_high, transfer_low, down_high, down_low,
    choose, outgoing, received, top_row, tops, picked_high, picked_low,
    load_sem, send_sem, recv_sem, top_send_sem, top_recv_sem,
):
    n_gx, n_gy, n_gz = sizes
    devices = n_gx * n_gy * n_gz
    coefs, cell_count = leaf.shape[0], leaf.shape[1] // 8
    ops = transfer.shape[0]
    slots = cells.shape[1]
    rows = cell_count + n_gz * slots
    i_gx, i_gy, i_gz = lax.axis_index("gx"), lax.axis_index("gy"), lax.axis_index("gz")

    def peer(x):
        return (
            xor(i_gx, x // (n_gz * n_gy), n_gx),
            xor(i_gy, (x // n_gz) % n_gy, n_gy),
            xor(i_gz, x % n_gz, n_gz),
        )

    def each(low, high, body):
        if devices <= 64:
            for x in range(low, high):
                body(x)
        else:
            lax.fori_loop(low, high, lambda x, c: (body(x), c)[1], 0)

    loads = [
        pltpu.make_async_copy(src, dst, load_sem.at[i])
        for i, (src, dst) in enumerate(
            [
                (leaf_hbm, leaf),
                (up_hbm, up),
                (cells_hbm.at[0], cells),
                (sends_hbm, sends),
                (source_hbm.at[0], source),
                (target_hbm.at[0], target),
                (counts_hbm, counts),
                (transfer_hbm, transfer),
                (down_hbm, down),
            ]
        )
    ]
    for load in loads:
        load.start()

    barrier = pltpu.get_barrier_semaphore()
    each(
        1,
        devices,
        lambda x: pl.semaphore_signal(barrier, inc=1, device_id=peer(x), device_id_type=MESH),
    )

    loads[2].wait()
    loads[3].wait()
    lane = lax.broadcasted_iota(jnp.int32, (1, slots), 1)
    wanted = jnp.concatenate(
        [
            jnp.where(lane < sends[0:1, s : s + 1], cells[s : s + 1, :], -1)
            for s in range(n_gz)
        ],
        axis=1,
    )
    pick = equal(wanted, cell_count)

    loads[0].wait()
    wide = lax.broadcasted_iota(jnp.int32, (128, 128), 1)
    tall = lax.broadcasted_iota(jnp.int32, (128, 128), 0)
    group = jnp.where(wide == tall % 16 * 8 + tall // 16, 1.0, 0.0).astype(BF16)
    for j in range(cell_count // 16):
        for part, held in zip(split(leaf[:, 128 * j : 128 * j + 128]), (leaf_high, leaf_low)):
            turned = lax.dot_general(group, part, NT, preferred_element_type=F32).astype(BF16)
            for k in range(8):
                held[k, 16 * j : 16 * j + 16, :] = turned[16 * k : 16 * k + 16]
    loads[1].wait()
    cell = jnp.zeros((cell_count, coefs), F32)
    for k in range(8):
        cell = cell + dot3((leaf_high[k], leaf_low[k]), split(up[k]))
    cell_high, cell_low = split(cell)
    out_rows = lax.dot_general(pick, cell_high, TN, preferred_element_type=F32) + lax.dot_general(
        pick, cell_low, TN, preferred_element_type=F32
    )
    outgoing[...] = out_rows.reshape(n_gz, slots, coefs)
    pl.semaphore_wait(barrier, devices - 1)

    def cell_copy(x):
        to = peer(x)
        return pltpu.make_async_remote_copy(
            src_ref=outgoing.at[to[2]],
            dst_ref=received.at[i_gz],
            send_sem=send_sem.at[x],
            recv_sem=recv_sem.at[x],
            device_id=to,
            device_id_type=MESH,
        )

    cell_copies = [cell_copy(x) for x in range(1, n_gz)]
    for copy in cell_copies:
        copy.start()

    octants = cell.reshape(cell_count // 8, 8, coefs).sum(0).T
    top = jnp.zeros((coefs, coefs), F32)
    for k in range(8):
        top = top + octants[:, k : k + 1] * up[k]
    top_row[...] = (8.0 / cell_count) ** 0.5 * top.sum(0, keepdims=True)

    def send_top(x):
        pltpu.make_async_remote_copy(
            src_ref=top_row,
            dst_ref=tops.at[x],
            send_sem=top_send_sem,
            recv_sem=top_recv_sem,
            device_id=peer(x),
            device_id_type=MESH,
        ).start()

    each(n_gz, devices, send_top)

    for load in loads[4:7]:
        load.wait()
    lane = lax.broadcasted_iota(jnp.int32, (1, target.shape[1]), 1)
    for k in range(ops):
        used = jnp.where(lane < counts[0:1, k : k + 1], target[k : k + 1, :], -1)
        choose[pl.ds(k * cell_count, cell_count), :] = lax.dot_general(
            equal(used, cell_count),
            equal(source[k : k + 1, :], rows),
            NT,
            preferred_element_type=F32,
        ).astype(BF16)

    loads[7].wait()
    for k in range(ops):
        transfer_high[k], transfer_low[k] = split(transfer[k])
    loads[8].wait()
    for k in range(8):
        down_high[k], down_low[k] = split(down[k])
    received[i_gz] = outgoing[i_gz]

    for copy in cell_copies:
        copy.wait_recv()
    got_high, got_low = split(received[...].reshape(n_gz * slots, coefs))
    table_high = jnp.concatenate([cell_high, got_high], axis=0)
    table_low = jnp.concatenate([cell_low, got_low], axis=0)
    for k in range(ops):
        chosen = choose[pl.ds(k * cell_count, cell_count), :]
        picked_high[k, 0:cell_count, :] = dot(chosen, table_high).astype(BF16)
        picked_low[k, 0:cell_count, :] = dot(chosen, table_low).astype(BF16)

    total = jnp.zeros((cell_count, coefs), F32)
    for k in range(ops):
        total = total + dot3(
            (picked_high[k], picked_low[k]), (transfer_high[k], transfer_low[k])
        )

    far = tops.at[pl.ds(n_gz, devices - n_gz)]
    pltpu.make_async_copy(far, far, top_recv_sem).wait()
    far_rows = []
    for k in range(ops):
        row = jnp.zeros((1, coefs), F32)
        for x in range(k, devices, ops):
            if x >= n_gz:
                row = row + tops[x]
        far_rows.append(row)
    far_columns = jnp.concatenate(far_rows, axis=0).T
    coarse = jnp.zeros((coefs, coefs), F32)
    for k in range(ops):
        coarse = coarse + far_columns[:, k : k + 1] * transfer[k]
    coarse = (32.0 / devices) ** 0.5 * coarse.sum(0, keepdims=True)
    column = jnp.broadcast_to(coarse, (8, coefs)).T[:, 0:1]
    coarse_down = jnp.concatenate(
        [(column * down[k]).sum(0, keepdims=True) for k in range(8)], axis=0
    )
    near = total.reshape(cell_count // 8, 8, coefs)
    local_cells = split((near + coarse_down[None]).reshape(cell_count, coefs))
    for k in range(8):
        out_ref[:, k, :] = dot3(local_cells, (down_high[k], down_low[k]))

    for copy in cell_copies:
        copy.wait_send()
    pltpu.make_async_copy(far, far, top_send_sem).wait()


def local(sizes, leaf_multipoles, upward_ops, transfer_ops, downward_ops, *lists):
    leaves, coefs = leaf_multipoles.shape
    cell_count = leaves // 8
    ops = transfer_ops.shape[0]
    send_cells, send_count, list_source, list_target, list_count = lists
    n_gz, slots = send_cells.shape[1:]
    devices = sizes[0] * sizes[1] * sizes[2]
    rows = cell_count + n_gz * slots
    vmem = pltpu.VMEM
    weights = lambda n: [vmem((n, coefs, coefs), BF16)] * 2
    out = pl.pallas_call(
        functools.partial(kernel, sizes),
        out_shape=jax.ShapeDtypeStruct((cell_count, 8, coefs), F32),
        in_specs=[pl.BlockSpec(memory_space=pl.ANY)] * 9,
        out_specs=pl.BlockSpec(memory_space=pltpu.VMEM),
        scratch_shapes=[
            vmem((coefs, leaves), F32),
            vmem(upward_ops.shape, F32),
            vmem(transfer_ops.shape, F32),
            vmem(downward_ops.shape, F32),
            vmem(send_cells.shape[1:], jnp.int32),
            vmem(send_count.shape, jnp.int32),
            vmem(list_source.shape[1:], jnp.int32),
            vmem(list_target.shape[1:], jnp.int32),
            vmem(list_count.shape, jnp.int32),
            *[vmem((8, cell_count, coefs), BF16)] * 2,
            *weights(ops),
            *weights(8),
            vmem((ops * cell_count, rows), BF16),
            vmem((n_gz, slots, coefs), F32),
            vmem((n_gz, slots, coefs), F32),
            vmem((1, coefs), F32),
            vmem((devices, 1, coefs), F32),
            *[vmem((ops, cell_count, coefs), BF16)] * 2,
            pltpu.SemaphoreType.DMA((9,)),
            pltpu.SemaphoreType.DMA((n_gz,)),
            pltpu.SemaphoreType.DMA((n_gz,)),
            pltpu.SemaphoreType.DMA,
            pltpu.SemaphoreType.DMA,
        ],
        compiler_params=pltpu.CompilerParams(
            collective_id=0, has_side_effects=True, vmem_limit_bytes=63 << 20
        ),
        cost_estimate=pl.CostEstimate(
            flops=6 * 2 * 32 * cell_count * coefs * coefs,
            bytes_accessed=8_000_000,
            transcendentals=0,
        ),
    )(leaf_multipoles.T, upward_ops, transfer_ops, downward_ops, *lists)
    return out.reshape(leaves, coefs)


def solution(mesh):
    sizes = tuple(mesh.shape[name] for name in ("gx", "gy", "gz"))
    split_all = ("gx", "gy", "gz")
    return jax.shard_map(
        functools.partial(local, sizes),
        mesh=mesh,
        in_specs=(
            P(split_all, None),
            P(),
            P(),
            P(),
            P(split_all, None, None),
            P(split_all, None),
            P(split_all, None, None),
            P(split_all, None, None),
            P(split_all, None),
        ),
        out_specs=P(split_all, None),
        check_vma=False,
    )
```

```python
import functools

import jax
import jax.numpy as jnp
from jax import lax
from jax.experimental import pallas as pl
from jax.experimental.pallas import tpu as pltpu
from jax.sharding import PartitionSpec as P

MESH = pl.DeviceIdType.MESH
F32 = jnp.float32
BF16 = jnp.bfloat16
NT = (((1,), (1,)), ((), ()))
TN = (((0,), (0,)), ((), ()))


def split(value):
    high = value.astype(BF16)
    return high, (value - high.astype(F32)).astype(BF16)


def dot(a, b):
    return jnp.dot(a, b, preferred_element_type=F32)


def dot3(both, high, low):
    half = both.shape[0] // 2
    wide = dot(both, high)
    return wide[:half] + wide[half:] + dot(both[:half], low)


def xor(a, b, size):
    total, bit = 0, 1
    while bit < size:
        total = total + ((a // bit + b // bit) % 2) * bit
        bit *= 2
    return total


def equal(row, length):
    rows = lax.broadcasted_iota(jnp.int32, (length, row.shape[1]), 0)
    return jnp.where(rows == row, 1.0, 0.0).astype(BF16)


def kernel(
    sizes,
    leaf_hbm, up_hbm, transfer_hbm, down_hbm,
    cells_hbm, sends_hbm, source_hbm, target_hbm, counts_hbm,
    out_ref,
    leaf, up, transfer, down,
    cells, sends, source, target, counts,
    leaf_both, transfer_high, transfer_low, down_high, down_low,
    choose, outgoing, received, top_row, tops, picked, staged,
    load_sem, send_sem, recv_sem, top_send_sem, top_recv_sem,
):
    n_gx, n_gy, n_gz = sizes
    devices = n_gx * n_gy * n_gz
    coefs, cell_count = leaf.shape[0], leaf.shape[1] // 8
    ops = transfer.shape[0]
    slots = cells.shape[1]
    rows = cell_count + n_gz * slots
    i_gx, i_gy, i_gz = lax.axis_index("gx"), lax.axis_index("gy"), lax.axis_index("gz")

    def peer(x):
        return (
            xor(i_gx, x // (n_gz * n_gy), n_gx),
            xor(i_gy, (x // n_gz) % n_gy, n_gy),
            xor(i_gz, x % n_gz, n_gz),
        )

    def each(low, high, body):
        if devices <= 64:
            for x in range(low, high):
                body(x)
        else:
            lax.fori_loop(low, high, lambda x, c: (body(x), c)[1], 0)

    loads = [
        pltpu.make_async_copy(src, dst, load_sem.at[i])
        for i, (src, dst) in enumerate(
            [
                (leaf_hbm, leaf),
                (up_hbm, up),
                (cells_hbm.at[0], cells),
                (sends_hbm, sends),
                (source_hbm.at[0], source),
                (target_hbm.at[0], target),
                (counts_hbm, counts),
                (transfer_hbm, transfer),
                (down_hbm, down),
            ]
        )
    ]
    for load in loads:
        load.start()

    barrier = pltpu.get_barrier_semaphore()
    each(
        1,
        devices,
        lambda x: pl.semaphore_signal(barrier, inc=1, device_id=peer(x), device_id_type=MESH),
    )

    loads[2].wait()
    loads[3].wait()
    lane = lax.broadcasted_iota(jnp.int32, (1, slots), 1)
    wanted = jnp.concatenate(
        [
            jnp.where(lane < sends[0:1, s : s + 1], cells[s : s + 1, :], -1)
            for s in range(n_gz)
        ],
        axis=1,
    )
    pick = equal(wanted, cell_count)

    loads[0].wait()
    wide = lax.broadcasted_iota(jnp.int32, (128, 128), 1)
    tall = lax.broadcasted_iota(jnp.int32, (128, 128), 0)
    group = jnp.where(wide == tall % 16 * 8 + tall // 16, 1.0, 0.0).astype(BF16)
    for j in range(cell_count // 16):
        for part, first in zip(split(leaf[:, 128 * j : 128 * j + 128]), (0, cell_count)):
            turned = lax.dot_general(group, part, NT, preferred_element_type=F32).astype(BF16)
            for k in range(8):
                leaf_both[
                    first + 16 * j : first + 16 * j + 16, coefs * k : coefs * k + coefs
                ] = turned[16 * k : 16 * k + 16]
    loads[1].wait()
    cell = dot3(leaf_both[...], *split(up[...].reshape(8 * coefs, coefs)))
    cell_high, cell_low = split(cell)
    out_rows = lax.dot_general(pick, cell_high, TN, preferred_element_type=F32) + lax.dot_general(
        pick, cell_low, TN, preferred_element_type=F32
    )
    outgoing[...] = out_rows.reshape(n_gz, slots, coefs)
    pl.semaphore_wait(barrier, devices - 1)

    def cell_copy(x):
        to = peer(x)
        return pltpu.make_async_remote_copy(
            src_ref=outgoing.at[to[2]],
            dst_ref=received.at[i_gz],
            send_sem=send_sem.at[x],
            recv_sem=recv_sem.at[x],
            device_id=to,
            device_id_type=MESH,
        )

    cell_copies = [cell_copy(x) for x in range(1, n_gz)]
    for copy in cell_copies:
        copy.start()

    octants = cell.reshape(cell_count // 8, 8, coefs).sum(0).T
    top = jnp.zeros((coefs, coefs), F32)
    for k in range(8):
        top = top + octants[:, k : k + 1] * up[k]
    top_row[...] = (8.0 / cell_count) ** 0.5 * top.sum(0, keepdims=True)

    def send_top(x):
        pltpu.make_async_remote_copy(
            src_ref=top_row,
            dst_ref=tops.at[x],
            send_sem=top_send_sem,
            recv_sem=top_recv_sem,
            device_id=peer(x),
            device_id_type=MESH,
        ).start()

    each(n_gz, devices, send_top)

    for load in loads[4:7]:
        load.wait()
    lane = lax.broadcasted_iota(jnp.int32, (1, target.shape[1]), 1)
    for k in range(ops):
        used = jnp.where(lane < counts[0:1, k : k + 1], target[k : k + 1, :], -1)
        choose[pl.ds(k * cell_count, cell_count), :] = lax.dot_general(
            equal(used, cell_count),
            equal(source[k : k + 1, :], rows),
            NT,
            preferred_element_type=F32,
        ).astype(BF16)

    loads[7].wait()
    transfer_high[...], transfer_low[...] = split(transfer[...].reshape(ops * coefs, coefs))
    loads[8].wait()
    for k in range(8):
        down_high[k], down_low[k] = split(down[k])
    received[i_gz] = outgoing[i_gz]

    for copy in cell_copies:
        copy.wait_recv()
    got_high, got_low = split(received[...].reshape(n_gz * slots, coefs))
    table_high = jnp.concatenate([cell_high, got_high], axis=0)
    table_low = jnp.concatenate([cell_low, got_low], axis=0)
    step = 4 * cell_count
    for part, first in ((table_high, 0), (table_low, cell_count)):
        for start in range(0, ops * cell_count, step):
            rows_picked = dot(choose[start : start + step, :], part).astype(BF16)
            for k in range(4):
                lane = coefs * (start // cell_count + k)
                picked[first : first + cell_count, lane : lane + coefs] = rows_picked[
                    cell_count * k : cell_count * k + cell_count
                ]
    total = dot3(picked[...], transfer_high[...], transfer_low[...])

    far = tops.at[pl.ds(n_gz, devices - n_gz)]
    pltpu.make_async_copy(far, far, top_recv_sem).wait()
    far_rows = []
    for k in range(ops):
        row = jnp.zeros((1, coefs), F32)
        for x in range(k, devices, ops):
            if x >= n_gz:
                row = row + tops[x]
        far_rows.append(row)
    far_columns = jnp.concatenate(far_rows, axis=0).T
    coarse = jnp.zeros((coefs, coefs), F32)
    for k in range(ops):
        coarse = coarse + far_columns[:, k : k + 1] * transfer[k]
    coarse = (32.0 / devices) ** 0.5 * coarse.sum(0, keepdims=True)
    column = jnp.broadcast_to(coarse, (8, coefs)).T[:, 0:1]
    coarse_down = jnp.concatenate(
        [(column * down[k]).sum(0, keepdims=True) for k in range(8)], axis=0
    )
    near = total.reshape(cell_count // 8, 8, coefs)
    local_cells = (near + coarse_down[None]).reshape(cell_count, coefs)
    both = jnp.concatenate(split(local_cells), axis=0)
    for k in range(8):
        staged[:, k, :] = dot3(both, down_high[k], down_low[k])
    same = equal(lax.broadcasted_iota(jnp.int32, (1, coefs), 1), coefs)
    for j in range(cell_count // 32):
        high, low = split(staged[32 * j : 32 * j + 32].reshape(256, coefs))
        out_ref[:, 256 * j : 256 * j + 256] = lax.dot_general(
            same, high, NT, preferred_element_type=F32
        ) + lax.dot_general(same, low, NT, preferred_element_type=F32)

    for copy in cell_copies:
        copy.wait_send()
    pltpu.make_async_copy(far, far, top_send_sem).wait()


def local(sizes, leaf_multipoles, upward_ops, transfer_ops, downward_ops, *lists):
    leaves, coefs = leaf_multipoles.shape
    cell_count = leaves // 8
    ops = transfer_ops.shape[0]
    send_cells, send_count, list_source, list_target, list_count = lists
    n_gz, slots = send_cells.shape[1:]
    devices = sizes[0] * sizes[1] * sizes[2]
    rows = cell_count + n_gz * slots
    vmem = pltpu.VMEM
    weights = lambda n: [vmem((n, coefs, coefs), BF16)] * 2
    out = pl.pallas_call(
        functools.partial(kernel, sizes),
        out_shape=jax.ShapeDtypeStruct((coefs, leaves), F32),
        in_specs=[pl.BlockSpec(memory_space=pltpu.HBM)] * 9,
        out_specs=pl.BlockSpec(memory_space=pltpu.VMEM),
        scratch_shapes=[
            vmem((coefs, leaves), F32),
            vmem(upward_ops.shape, F32),
            vmem(transfer_ops.shape, F32),
            vmem(downward_ops.shape, F32),
            vmem(send_cells.shape[1:], jnp.int32),
            vmem(send_count.shape, jnp.int32),
            vmem(list_source.shape[1:], jnp.int32),
            vmem(list_target.shape[1:], jnp.int32),
            vmem(list_count.shape, jnp.int32),
            vmem((2 * cell_count, 8 * coefs), BF16),
            *[vmem((ops * coefs, coefs), BF16)] * 2,
            *weights(8),
            vmem((ops * cell_count, rows), BF16),
            vmem((n_gz, slots, coefs), F32),
            vmem((n_gz, slots, coefs), F32),
            vmem((1, coefs), F32),
            vmem((devices, 1, coefs), F32),
            vmem((2 * cell_count, ops * coefs), BF16),
            vmem((cell_count, 8, coefs), F32),
            pltpu.SemaphoreType.DMA((9,)),
            pltpu.SemaphoreType.DMA((n_gz,)),
            pltpu.SemaphoreType.DMA((n_gz,)),
            pltpu.SemaphoreType.DMA,
            pltpu.SemaphoreType.DMA,
        ],
        compiler_params=pltpu.CompilerParams(
            collective_id=0, has_side_effects=True, vmem_limit_bytes=53 << 20
        ),
        cost_estimate=pl.CostEstimate(
            flops=6 * 2 * 32 * cell_count * coefs * coefs,
            bytes_accessed=8_000_000,
            transcendentals=0,
        ),
    )(leaf_multipoles.T, upward_ops, transfer_ops, downward_ops, *lists)
    return out.T


def solution(mesh):
    sizes = tuple(mesh.shape[name] for name in ("gx", "gy", "gz"))
    split_all = ("gx", "gy", "gz")
    return jax.shard_map(
        functools.partial(local, sizes),
        mesh=mesh,
        in_specs=(
            P(split_all, None),
            P(),
            P(),
            P(),
            P(split_all, None, None),
            P(split_all, None),
            P(split_all, None, None),
            P(split_all, None, None),
            P(split_all, None),
        ),
        out_specs=P(split_all, None),
        check_vma=False,
    )
```

```python
import functools

import jax
import jax.numpy as jnp
from jax import lax
from jax.experimental import pallas as pl
from jax.experimental.pallas import tpu as pltpu
from jax.sharding import PartitionSpec as P

MESH = pl.DeviceIdType.MESH
F32 = jnp.float32
BF16 = jnp.bfloat16
NT = (((1,), (1,)), ((), ()))
TN = (((0,), (0,)), ((), ()))


def split(value):
    high = value.astype(BF16)
    return high, (value - high.astype(F32)).astype(BF16)


def dot(a, b):
    return jnp.dot(a, b, preferred_element_type=F32)


def dot3(both, high, low):
    half = both.shape[0] // 2
    wide = dot(both, high)
    return wide[:half] + wide[half:] + dot(both[:half], low)


def xor(a, b, size):
    total, bit = 0, 1
    while bit < size:
        total = total + ((a // bit + b // bit) % 2) * bit
        bit *= 2
    return total


def equal(row, length):
    rows = lax.broadcasted_iota(jnp.int32, (length, row.shape[1]), 0)
    return jnp.where(rows == row, 1.0, 0.0).astype(BF16)


def kernel(
    sizes,
    leaf_hbm, up_hbm, transfer_hbm, down_hbm,
    cells_hbm, sends_hbm, source_hbm, target_hbm, counts_hbm,
    out_ref,
    leaf, up, transfer, down,
    cells, sends, source, target, counts,
    leaf_both, transfer_high, transfer_low, down_high, down_low,
    choose, outgoing, received, top_row, tops, picked, staged,
    load_sem, send_sem, recv_sem, top_send_sem, top_recv_sem,
):
    n_gx, n_gy, n_gz = sizes
    devices = n_gx * n_gy * n_gz
    coefs, cell_count = leaf.shape[0], leaf.shape[1] // 8
    ops = transfer.shape[0]
    slots = cells.shape[1]
    rows = cell_count + n_gz * slots
    i_gx, i_gy, i_gz = lax.axis_index("gx"), lax.axis_index("gy"), lax.axis_index("gz")

    def peer(x):
        return (
            xor(i_gx, x // (n_gz * n_gy), n_gx),
            xor(i_gy, (x // n_gz) % n_gy, n_gy),
            xor(i_gz, x % n_gz, n_gz),
        )

    def each(low, high, body):
        if devices <= 64:
            for x in range(low, high):
                body(x)
        else:
            lax.fori_loop(low, high, lambda x, c: (body(x), c)[1], 0)

    loads = [
        pltpu.make_async_copy(src, dst, load_sem.at[i])
        for i, (src, dst) in enumerate(
            [
                (leaf_hbm, leaf),
                (up_hbm, up),
                (cells_hbm.at[0], cells),
                (sends_hbm, sends),
                (source_hbm.at[0], source),
                (target_hbm.at[0], target),
                (counts_hbm, counts),
                (transfer_hbm, transfer),
                (down_hbm, down),
            ]
        )
    ]
    for load in loads:
        load.start()

    barrier = pltpu.get_barrier_semaphore()
    each(
        1,
        devices,
        lambda x: pl.semaphore_signal(barrier, inc=1, device_id=peer(x), device_id_type=MESH),
    )

    loads[2].wait()
    loads[3].wait()
    lane = lax.broadcasted_iota(jnp.int32, (1, slots), 1)
    wanted = jnp.concatenate(
        [
            jnp.where(lane < sends[0:1, s : s + 1], cells[s : s + 1, :], -1)
            for s in range(n_gz)
        ],
        axis=1,
    )
    pick = equal(wanted, cell_count)

    loads[0].wait()
    wide = lax.broadcasted_iota(jnp.int32, (128, 128), 1)
    tall = lax.broadcasted_iota(jnp.int32, (128, 128), 0)
    group = jnp.where(wide == tall % 16 * 8 + tall // 16, 1.0, 0.0).astype(BF16)
    for j in range(cell_count // 16):
        for part, first in zip(split(leaf[:, 128 * j : 128 * j + 128]), (0, cell_count)):
            turned = lax.dot_general(group, part, NT, preferred_element_type=F32).astype(BF16)
            for k in range(8):
                leaf_both[
                    first + 16 * j : first + 16 * j + 16, coefs * k : coefs * k + coefs
                ] = turned[16 * k : 16 * k + 16]
    loads[1].wait()
    cell = dot3(leaf_both[...], *split(up[...].reshape(8 * coefs, coefs)))
    cell_high, cell_low = split(cell)
    out_rows = lax.dot_general(pick, cell_high, TN, preferred_element_type=F32) + lax.dot_general(
        pick, cell_low, TN, preferred_element_type=F32
    )
    outgoing[...] = out_rows.reshape(n_gz, slots, coefs)
    pl.semaphore_wait(barrier, devices - 1)

    def cell_copy(x):
        to = peer(x)
        return pltpu.make_async_remote_copy(
            src_ref=outgoing.at[to[2]],
            dst_ref=received.at[i_gz],
            send_sem=send_sem.at[x],
            recv_sem=recv_sem.at[x],
            device_id=to,
            device_id_type=MESH,
        )

    cell_copies = [cell_copy(x) for x in range(1, n_gz)]
    for copy in cell_copies:
        copy.start()

    octants = cell.reshape(cell_count // 8, 8, coefs).sum(0).T
    top = jnp.zeros((coefs, coefs), F32)
    for k in range(8):
        top = top + octants[:, k : k + 1] * up[k]
    top_row[...] = (8.0 / cell_count) ** 0.5 * top.sum(0, keepdims=True)

    def send_top(x):
        pltpu.make_async_remote_copy(
            src_ref=top_row,
            dst_ref=tops.at[x],
            send_sem=top_send_sem,
            recv_sem=top_recv_sem,
            device_id=peer(x),
            device_id_type=MESH,
        ).start()

    each(n_gz, devices, send_top)

    for load in loads[4:7]:
        load.wait()
    lane = lax.broadcasted_iota(jnp.int32, (1, target.shape[1]), 1)
    for k in range(ops):
        used = jnp.where(lane < counts[0:1, k : k + 1], target[k : k + 1, :], -1)
        choose[pl.ds(k * cell_count, cell_count), :] = lax.dot_general(
            equal(used, cell_count),
            equal(source[k : k + 1, :], rows),
            NT,
            preferred_element_type=F32,
        ).astype(BF16)

    loads[7].wait()
    transfer_high[...], transfer_low[...] = split(transfer[...].reshape(ops * coefs, coefs))
    loads[8].wait()
    for k in range(8):
        down_high[k], down_low[k] = split(down[k])
    received[i_gz] = outgoing[i_gz]

    for copy in cell_copies:
        copy.wait_recv()
    got_high, got_low = split(received[...].reshape(n_gz * slots, coefs))
    table_high = jnp.concatenate([cell_high, got_high], axis=0)
    table_low = jnp.concatenate([cell_low, got_low], axis=0)
    step = 4 * cell_count
    for part, first in ((table_high, 0), (table_low, cell_count)):
        for start in range(0, ops * cell_count, step):
            rows_picked = dot(choose[start : start + step, :], part).astype(BF16)
            for k in range(4):
                lane = coefs * (start // cell_count + k)
                picked[first : first + cell_count, lane : lane + coefs] = rows_picked[
                    cell_count * k : cell_count * k + cell_count
                ]
    total = dot3(picked[...], transfer_high[...], transfer_low[...])

    far = tops.at[pl.ds(n_gz, devices - n_gz)]
    pltpu.make_async_copy(far, far, top_recv_sem).wait()
    far_rows = []
    for k in range(ops):
        row = jnp.zeros((1, coefs), F32)
        for x in range(k, devices, ops):
            if x >= n_gz:
                row = row + tops[x]
        far_rows.append(row)
    far_columns = jnp.concatenate(far_rows, axis=0).T
    coarse = jnp.zeros((coefs, coefs), F32)
    for k in range(ops):
        coarse = coarse + far_columns[:, k : k + 1] * transfer[k]
    coarse = (32.0 / devices) ** 0.5 * coarse.sum(0, keepdims=True)
    column = jnp.broadcast_to(coarse, (8, coefs)).T[:, 0:1]
    coarse_down = jnp.concatenate(
        [(column * down[k]).sum(0, keepdims=True) for k in range(8)], axis=0
    )
    near = total.reshape(cell_count // 8, 8, coefs)
    local_cells = (near + coarse_down[None]).reshape(cell_count, coefs)
    both = jnp.concatenate(split(local_cells), axis=0)
    for k in range(8):
        staged[:, k, :] = dot3(both, down_high[k], down_low[k])
    same = equal(lax.broadcasted_iota(jnp.int32, (1, coefs), 1), coefs)
    for j in range(cell_count // 32):
        high, low = split(staged[32 * j : 32 * j + 32].reshape(256, coefs))
        out_ref[:, 256 * j : 256 * j + 256] = lax.dot_general(
            same, high, NT, preferred_element_type=F32
        ) + lax.dot_general(same, low, NT, preferred_element_type=F32)

    for copy in cell_copies:
        copy.wait_send()
    pltpu.make_async_copy(far, far, top_send_sem).wait()


def local(sizes, leaf_multipoles, upward_ops, transfer_ops, downward_ops, *lists):
    leaves, coefs = leaf_multipoles.shape
    cell_count = leaves // 8
    ops = transfer_ops.shape[0]
    send_cells, send_count, list_source, list_target, list_count = lists
    n_gz, slots = send_cells.shape[1:]
    devices = sizes[0] * sizes[1] * sizes[2]
    rows = cell_count + n_gz * slots
    vmem = pltpu.VMEM
    weights = lambda n: [vmem((n, coefs, coefs), BF16)] * 2
    operands = (leaf_multipoles.T, upward_ops, transfer_ops, downward_ops, *lists)
    out = pl.pallas_call(
        functools.partial(kernel, sizes),
        out_shape=jax.ShapeDtypeStruct((coefs, leaves), F32),
        in_specs=[pl.BlockSpec(memory_space=pltpu.HBM)] * 9,
        out_specs=pl.BlockSpec(memory_space=pltpu.VMEM),
        scratch_shapes=[
            vmem((coefs, leaves), F32),
            vmem(upward_ops.shape, F32),
            vmem(transfer_ops.shape, F32),
            vmem(downward_ops.shape, F32),
            vmem(send_cells.shape[1:], jnp.int32),
            vmem(send_count.shape, jnp.int32),
            vmem(list_source.shape[1:], jnp.int32),
            vmem(list_target.shape[1:], jnp.int32),
            vmem(list_count.shape, jnp.int32),
            vmem((2 * cell_count, 8 * coefs), BF16),
            *[vmem((ops * coefs, coefs), BF16)] * 2,
            *weights(8),
            vmem((ops * cell_count, rows), BF16),
            vmem((n_gz, slots, coefs), F32),
            vmem((n_gz, slots, coefs), F32),
            vmem((1, coefs), F32),
            vmem((devices, 1, coefs), F32),
            vmem((2 * cell_count, ops * coefs), BF16),
            vmem((cell_count, 8, coefs), F32),
            pltpu.SemaphoreType.DMA((9,)),
            pltpu.SemaphoreType.DMA((n_gz,)),
            pltpu.SemaphoreType.DMA((n_gz,)),
            pltpu.SemaphoreType.DMA,
            pltpu.SemaphoreType.DMA,
        ],
        compiler_params=pltpu.CompilerParams(
            collective_id=0, has_side_effects=True, vmem_limit_bytes=48 << 20
        ),
        cost_estimate=pl.CostEstimate(
            flops=6 * 2 * 32 * cell_count * coefs * coefs,
            bytes_accessed=8_000_000,
            transcendentals=0,
        ),
    )(*(pltpu.with_memory_space_constraint(x, pltpu.HBM) for x in operands))
    return out.T


def solution(mesh):
    sizes = tuple(mesh.shape[name] for name in ("gx", "gy", "gz"))
    split_all = ("gx", "gy", "gz")
    return jax.shard_map(
        functools.partial(local, sizes),
        mesh=mesh,
        in_specs=(
            P(split_all, None),
            P(),
            P(),
            P(),
            P(split_all, None, None),
            P(split_all, None),
            P(split_all, None, None),
            P(split_all, None, None),
            P(split_all, None),
        ),
        out_specs=P(split_all, None),
        check_vma=False,
    )
```

```python
import functools

import jax
import jax.numpy as jnp
from jax import lax
from jax.experimental import pallas as pl
from jax.experimental.pallas import tpu as pltpu
from jax.sharding import PartitionSpec as P

MESH = pl.DeviceIdType.MESH
F32 = jnp.float32
BF16 = jnp.bfloat16
NT = (((1,), (1,)), ((), ()))
TN = (((0,), (0,)), ((), ()))


def split(value):
    high = value.astype(BF16)
    return high, (value - high.astype(F32)).astype(BF16)


def dot(a, b):
    return jnp.dot(a, b, preferred_element_type=F32)


def dot3(both, high, low):
    half = both.shape[0] // 2
    wide = dot(both, high)
    return wide[:half] + wide[half:] + dot(both[:half], low)


def flips(place, size):
    bits = []
    while 1 << len(bits) < size:
        bit = 1 << len(bits)
        bits.append(bit - 2 * bit * lax.rem(lax.div(place, bit), 2))
    return bits


def xor(place, bits, x):
    for i, step in enumerate(bits):
        if isinstance(x, int):
            place = place + step if x >> i & 1 else place
        else:
            place = place + step * lax.rem(lax.div(x, 1 << i), 2)
    return place


def equal(row, length):
    rows = lax.broadcasted_iota(jnp.int32, (length, row.shape[1]), 0)
    return jnp.where(rows == row, 1.0, 0.0).astype(BF16)


def kernel(
    sizes,
    leaf_hbm, up_hbm, transfer_hbm, down_hbm,
    cells_hbm, sends_hbm, source_hbm, target_hbm, counts_hbm,
    out_ref,
    leaf, up, transfer, down,
    cells, sends, source, target, counts,
    leaf_both, transfer_high, transfer_low, down_high, down_low,
    choose, outgoing, received, top_row, tops, picked, staged,
    load_sem, send_sem, recv_sem, top_send_sem, top_recv_sem,
):
    n_gx, n_gy, n_gz = sizes
    devices = n_gx * n_gy * n_gz
    coefs, cell_count = leaf.shape[0], leaf.shape[1] // 8
    ops = transfer.shape[0]
    slots = cells.shape[1]
    rows = cell_count + n_gz * slots
    i_gx, i_gy, i_gz = lax.axis_index("gx"), lax.axis_index("gy"), lax.axis_index("gz")

    places = [(i_gx, n_gx, n_gy * n_gz), (i_gy, n_gy, n_gz), (i_gz, n_gz, 1)]
    axes = [(place, flips(place, size), size, below) for place, size, below in places]
    known = [[xor(p, bits, v) for v in range(size)] for p, bits, size, _ in axes]

    def peer(x):
        if isinstance(x, int):
            return tuple(
                table[x // below % size] for table, (_, _, size, below) in zip(known, axes)
            )
        return tuple(
            xor(p, bits, lax.rem(lax.div(x, below), size)) for p, bits, size, below in axes
        )

    def each(low, high, body):
        if devices <= 64:
            for x in range(low, high):
                body(x)
        else:
            lax.fori_loop(low, high, lambda x, c: (body(x), c)[1], 0)

    loads = [
        pltpu.make_async_copy(src, dst, load_sem.at[i])
        for i, (src, dst) in enumerate(
            [
                (leaf_hbm, leaf),
                (up_hbm, up),
                (cells_hbm.at[0], cells),
                (sends_hbm, sends),
                (source_hbm.at[0], source),
                (target_hbm.at[0], target),
                (counts_hbm, counts),
                (transfer_hbm, transfer),
                (down_hbm, down),
            ]
        )
    ]
    for load in loads[:7]:
        load.start()

    barrier = pltpu.get_barrier_semaphore()
    each(
        1,
        devices,
        lambda x: pl.semaphore_signal(barrier, inc=1, device_id=peer(x), device_id_type=MESH),
    )

    loads[2].wait()
    loads[3].wait()
    lane = lax.broadcasted_iota(jnp.int32, (1, slots), 1)
    wanted = jnp.concatenate(
        [
            jnp.where(lane < sends[0:1, s : s + 1], cells[s : s + 1, :], -1)
            for s in range(n_gz)
        ],
        axis=1,
    )
    pick = equal(wanted, cell_count)

    loads[0].wait()
    loads[1].wait()
    loads[7].start()
    loads[8].start()
    wide = lax.broadcasted_iota(jnp.int32, (128, 128), 1)
    tall = lax.broadcasted_iota(jnp.int32, (128, 128), 0)
    group = jnp.where(wide == tall % 16 * 8 + tall // 16, 1.0, 0.0).astype(BF16)
    for j in range(cell_count // 16):
        for part, first in zip(split(leaf[:, 128 * j : 128 * j + 128]), (0, cell_count)):
            turned = lax.dot_general(group, part, NT, preferred_element_type=F32).astype(BF16)
            for k in range(8):
                leaf_both[
                    first + 16 * j : first + 16 * j + 16, coefs * k : coefs * k + coefs
                ] = turned[16 * k : 16 * k + 16]
    cell = dot3(leaf_both[...], *split(up[...].reshape(8 * coefs, coefs)))
    cell_high, cell_low = split(cell)
    out_rows = lax.dot_general(pick, cell_high, TN, preferred_element_type=F32) + lax.dot_general(
        pick, cell_low, TN, preferred_element_type=F32
    )
    outgoing[...] = out_rows.reshape(n_gz, slots, coefs)
    octants = cell.reshape(cell_count // 8, 8, coefs).sum(0).T
    top = jnp.zeros((coefs, coefs), F32)
    for k in range(8):
        top = top + octants[:, k : k + 1] * up[k]
    top_row[...] = (8.0 / cell_count) ** 0.5 * top.sum(0, keepdims=True)
    pl.semaphore_wait(barrier, devices - 1)

    def cell_copy(x):
        to = peer(x)
        return pltpu.make_async_remote_copy(
            src_ref=outgoing.at[to[2]],
            dst_ref=received.at[i_gz],
            send_sem=send_sem.at[x],
            recv_sem=recv_sem.at[x],
            device_id=to,
            device_id_type=MESH,
        )

    cell_copies = [cell_copy(x) for x in range(1, n_gz)]
    for copy in cell_copies:
        copy.start()

    def send_top(x):
        pltpu.make_async_remote_copy(
            src_ref=top_row,
            dst_ref=tops.at[x],
            send_sem=top_send_sem,
            recv_sem=top_recv_sem,
            device_id=peer(x),
            device_id_type=MESH,
        ).start()

    each(n_gz, devices, send_top)

    for load in loads[4:7]:
        load.wait()
    lane = lax.broadcasted_iota(jnp.int32, (1, target.shape[1]), 1)
    for k in range(ops):
        used = jnp.where(lane < counts[0:1, k : k + 1], target[k : k + 1, :], -1)
        choose[pl.ds(k * cell_count, cell_count), :] = lax.dot_general(
            equal(used, cell_count),
            equal(source[k : k + 1, :], rows),
            NT,
            preferred_element_type=F32,
        ).astype(BF16)

    loads[7].wait()
    transfer_high[...], transfer_low[...] = split(transfer[...].reshape(ops * coefs, coefs))
    loads[8].wait()
    for k in range(8):
        down_high[k], down_low[k] = split(down[k])
    received[i_gz] = outgoing[i_gz]

    for copy in cell_copies:
        copy.wait_recv()
    got_high, got_low = split(received[...].reshape(n_gz * slots, coefs))
    table_high = jnp.concatenate([cell_high, got_high], axis=0)
    table_low = jnp.concatenate([cell_low, got_low], axis=0)
    step = 4 * cell_count
    for part, first in ((table_high, 0), (table_low, cell_count)):
        for start in range(0, ops * cell_count, step):
            rows_picked = dot(choose[start : start + step, :], part).astype(BF16)
            for k in range(4):
                lane = coefs * (start // cell_count + k)
                picked[first : first + cell_count, lane : lane + coefs] = rows_picked[
                    cell_count * k : cell_count * k + cell_count
                ]
    total = dot3(picked[...], transfer_high[...], transfer_low[...])

    far = tops.at[pl.ds(n_gz, devices - n_gz)]
    pltpu.make_async_copy(far, far, top_recv_sem).wait()
    far_rows = []
    for k in range(ops):
        row = jnp.zeros((1, coefs), F32)
        for x in range(k, devices, ops):
            if x >= n_gz:
                row = row + tops[x]
        far_rows.append(row)
    far_columns = jnp.concatenate(far_rows, axis=0).T
    coarse = jnp.zeros((coefs, coefs), F32)
    for k in range(ops):
        coarse = coarse + far_columns[:, k : k + 1] * transfer[k]
    coarse = (32.0 / devices) ** 0.5 * coarse.sum(0, keepdims=True)
    column = jnp.broadcast_to(coarse, (8, coefs)).T[:, 0:1]
    coarse_down = jnp.concatenate(
        [(column * down[k]).sum(0, keepdims=True) for k in range(8)], axis=0
    )
    near = total.reshape(cell_count // 8, 8, coefs)
    local_cells = (near + coarse_down[None]).reshape(cell_count, coefs)
    both = jnp.concatenate(split(local_cells), axis=0)
    for k in range(8):
        staged[:, k, :] = dot3(both, down_high[k], down_low[k])
    same = equal(lax.broadcasted_iota(jnp.int32, (1, coefs), 1), coefs)
    for j in range(cell_count // 32):
        high, low = split(staged[32 * j : 32 * j + 32].reshape(256, coefs))
        out_ref[:, 256 * j : 256 * j + 256] = lax.dot_general(
            same, high, NT, preferred_element_type=F32
        ) + lax.dot_general(same, low, NT, preferred_element_type=F32)

    for copy in cell_copies:
        copy.wait_send()
    pltpu.make_async_copy(far, far, top_send_sem).wait()


def local(sizes, leaf_multipoles, upward_ops, transfer_ops, downward_ops, *lists):
    leaves, coefs = leaf_multipoles.shape
    cell_count = leaves // 8
    ops = transfer_ops.shape[0]
    send_cells, send_count, list_source, list_target, list_count = lists
    n_gz, slots = send_cells.shape[1:]
    devices = sizes[0] * sizes[1] * sizes[2]
    rows = cell_count + n_gz * slots
    vmem = pltpu.VMEM
    weights = lambda n: [vmem((n, coefs, coefs), BF16)] * 2
    operands = (leaf_multipoles.T, upward_ops, transfer_ops, downward_ops, *lists)
    out = pl.pallas_call(
        functools.partial(kernel, sizes),
        out_shape=jax.ShapeDtypeStruct((coefs, leaves), F32),
        in_specs=[pl.BlockSpec(memory_space=pltpu.HBM)] * 9,
        out_specs=pl.BlockSpec(memory_space=pltpu.VMEM),
        scratch_shapes=[
            vmem((coefs, leaves), F32),
            vmem(upward_ops.shape, F32),
            vmem(transfer_ops.shape, F32),
            vmem(downward_ops.shape, F32),
            vmem(send_cells.shape[1:], jnp.int32),
            vmem(send_count.shape, jnp.int32),
            vmem(list_source.shape[1:], jnp.int32),
            vmem(list_target.shape[1:], jnp.int32),
            vmem(list_count.shape, jnp.int32),
            vmem((2 * cell_count, 8 * coefs), BF16),
            *[vmem((ops * coefs, coefs), BF16)] * 2,
            *weights(8),
            vmem((ops * cell_count, rows), BF16),
            vmem((n_gz, slots, coefs), F32),
            vmem((n_gz, slots, coefs), F32),
            vmem((1, coefs), F32),
            vmem((devices, 1, coefs), F32),
            vmem((2 * cell_count, ops * coefs), BF16),
            vmem((cell_count, 8, coefs), F32),
            pltpu.SemaphoreType.DMA((9,)),
            pltpu.SemaphoreType.DMA((n_gz,)),
            pltpu.SemaphoreType.DMA((n_gz,)),
            pltpu.SemaphoreType.DMA,
            pltpu.SemaphoreType.DMA,
        ],
        compiler_params=pltpu.CompilerParams(
            collective_id=0, has_side_effects=True, vmem_limit_bytes=48 << 20
        ),
        cost_estimate=pl.CostEstimate(
            flops=6 * 2 * 32 * cell_count * coefs * coefs,
            bytes_accessed=8_000_000,
            transcendentals=0,
        ),
    )(*(pltpu.with_memory_space_constraint(x, pltpu.HBM) for x in operands))
    return out.T


def solution(mesh):
    sizes = tuple(mesh.shape[name] for name in ("gx", "gy", "gz"))
    split_all = ("gx", "gy", "gz")
    return jax.shard_map(
        functools.partial(local, sizes),
        mesh=mesh,
        in_specs=(
            P(split_all, None),
            P(),
            P(),
            P(),
            P(split_all, None, None),
            P(split_all, None),
            P(split_all, None, None),
            P(split_all, None, None),
            P(split_all, None),
        ),
        out_specs=P(split_all, None),
        check_vma=False,
    )
```

```python
import functools

import jax
import jax.numpy as jnp
from jax import lax
from jax.experimental import pallas as pl
from jax.experimental.pallas import tpu as pltpu
from jax.sharding import PartitionSpec as P

MESH = pl.DeviceIdType.MESH
F32 = jnp.float32
BF16 = jnp.bfloat16
NT = (((1,), (1,)), ((), ()))
TN = (((0,), (0,)), ((), ()))


def split(value):
    high = value.astype(BF16)
    return high, (value - high.astype(F32)).astype(BF16)


def dot(a, b):
    return jnp.dot(a, b, preferred_element_type=F32)


def dot3(both, high, low):
    half = both.shape[0] // 2
    wide = dot(both, high)
    return wide[:half] + wide[half:] + dot(both[:half], low)


def flips(place, size):
    bits = []
    while 1 << len(bits) < size:
        bit = 1 << len(bits)
        bits.append(bit - 2 * bit * lax.rem(lax.div(place, bit), 2))
    return bits


def xor(place, bits, x):
    for i, step in enumerate(bits):
        if isinstance(x, int):
            place = place + step if x >> i & 1 else place
        else:
            place = place + step * lax.rem(lax.div(x, 1 << i), 2)
    return place


def equal(row, length):
    rows = lax.broadcasted_iota(jnp.int32, (length, row.shape[1]), 0)
    return jnp.where(rows == row, 1.0, 0.0).astype(BF16)


def kernel(
    sizes,
    leaf_hbm, up_hbm, transfer_hbm, down_hbm,
    cells_hbm, sends_hbm, source_hbm, target_hbm, counts_hbm,
    out_ref,
    leaf, up, transfer, down,
    cells, sends, source, target, counts,
    leaf_both, transfer_high, transfer_low, down_high, down_low,
    choose, outgoing, received, top_row, tops, picked, staged,
    load_sem, send_sem, recv_sem, top_send_sem, top_recv_sem,
):
    n_gx, n_gy, n_gz = sizes
    devices = n_gx * n_gy * n_gz
    coefs, cell_count = leaf.shape[0], leaf.shape[1] // 8
    ops = transfer.shape[0]
    slots = cells.shape[1]
    rows = cell_count + n_gz * slots
    i_gx, i_gy, i_gz = lax.axis_index("gx"), lax.axis_index("gy"), lax.axis_index("gz")

    places = [(i_gx, n_gx, n_gy * n_gz), (i_gy, n_gy, n_gz), (i_gz, n_gz, 1)]
    axes = [(place, flips(place, size), size, below) for place, size, below in places]
    known = [[xor(p, bits, v) for v in range(size)] for p, bits, size, _ in axes]

    def peer(x):
        if isinstance(x, int):
            return tuple(
                table[x // below % size] for table, (_, _, size, below) in zip(known, axes)
            )
        return tuple(
            xor(p, bits, lax.rem(lax.div(x, below), size)) for p, bits, size, below in axes
        )

    def each(low, high, body):
        if devices <= 64:
            for x in range(low, high):
                body(x)
        else:
            lax.fori_loop(low, high, lambda x, c: (body(x), c)[1], 0)

    loads = [
        pltpu.make_async_copy(src, dst, load_sem.at[i])
        for i, (src, dst) in enumerate(
            [
                (leaf_hbm, leaf),
                (up_hbm, up),
                (cells_hbm.at[0], cells),
                (sends_hbm, sends),
                (source_hbm.at[0], source),
                (target_hbm.at[0], target),
                (counts_hbm, counts),
                (transfer_hbm, transfer),
                (down_hbm, down),
            ]
        )
    ]
    for load in loads[:7]:
        load.start()

    barrier = pltpu.get_barrier_semaphore()
    each(
        1,
        devices,
        lambda x: pl.semaphore_signal(barrier, inc=1, device_id=peer(x), device_id_type=MESH),
    )

    loads[2].wait()
    loads[3].wait()
    lane = lax.broadcasted_iota(jnp.int32, (1, slots), 1)
    wanted = jnp.concatenate(
        [
            jnp.where(lane < sends[0:1, s : s + 1], cells[s : s + 1, :], -1)
            for s in range(n_gz)
        ],
        axis=1,
    )
    pick = equal(wanted, cell_count)

    loads[0].wait()
    loads[1].wait()
    loads[7].start()
    loads[8].start()
    staged[...] = leaf[...].T.reshape(cell_count, 8, coefs)
    for k in range(8):
        lanes = slice(coefs * k, coefs * k + coefs)
        leaf_both[0:cell_count, lanes], leaf_both[cell_count:, lanes] = split(staged[:, k, :])
    cell = dot3(leaf_both[...], *split(up[...].reshape(8 * coefs, coefs)))
    cell_high, cell_low = split(cell)
    out_rows = lax.dot_general(pick, cell_high, TN, preferred_element_type=F32) + lax.dot_general(
        pick, cell_low, TN, preferred_element_type=F32
    )
    outgoing[...] = out_rows.reshape(n_gz, slots, coefs)
    octants = cell.reshape(cell_count // 8, 8, coefs).sum(0).T
    top = jnp.zeros((coefs, coefs), F32)
    for k in range(8):
        top = top + octants[:, k : k + 1] * up[k]
    top_row[...] = (8.0 / cell_count) ** 0.5 * top.sum(0, keepdims=True)
    pl.semaphore_wait(barrier, devices - 1)

    def cell_copy(x):
        to = peer(x)
        return pltpu.make_async_remote_copy(
            src_ref=outgoing.at[to[2]],
            dst_ref=received.at[i_gz],
            send_sem=send_sem.at[x],
            recv_sem=recv_sem.at[x],
            device_id=to,
            device_id_type=MESH,
        )

    cell_copies = [cell_copy(x) for x in range(1, n_gz)]
    for copy in cell_copies:
        copy.start()

    def send_top(x):
        pltpu.make_async_remote_copy(
            src_ref=top_row,
            dst_ref=tops.at[x],
            send_sem=top_send_sem,
            recv_sem=top_recv_sem,
            device_id=peer(x),
            device_id_type=MESH,
        ).start()

    each(n_gz, devices, send_top)

    for load in loads[4:7]:
        load.wait()
    lane = lax.broadcasted_iota(jnp.int32, (1, target.shape[1]), 1)
    for k in range(ops):
        used = jnp.where(lane < counts[0:1, k : k + 1], target[k : k + 1, :], -1)
        choose[pl.ds(k * cell_count, cell_count), :] = lax.dot_general(
            equal(used, cell_count),
            equal(source[k : k + 1, :], rows),
            NT,
            preferred_element_type=F32,
        ).astype(BF16)

    loads[7].wait()
    transfer_high[...], transfer_low[...] = split(transfer[...].reshape(ops * coefs, coefs))
    loads[8].wait()
    for k in range(8):
        down_high[k], down_low[k] = split(down[k])
    received[i_gz] = outgoing[i_gz]

    for copy in cell_copies:
        copy.wait_recv()
    got_high, got_low = split(received[...].reshape(n_gz * slots, coefs))
    table_high = jnp.concatenate([cell_high, got_high], axis=0)
    table_low = jnp.concatenate([cell_low, got_low], axis=0)
    step = 4 * cell_count
    for part, first in ((table_high, 0), (table_low, cell_count)):
        for start in range(0, ops * cell_count, step):
            rows_picked = dot(choose[start : start + step, :], part).astype(BF16)
            for k in range(4):
                lane = coefs * (start // cell_count + k)
                picked[first : first + cell_count, lane : lane + coefs] = rows_picked[
                    cell_count * k : cell_count * k + cell_count
                ]
    total = dot3(picked[...], transfer_high[...], transfer_low[...])

    far = tops.at[pl.ds(n_gz, devices - n_gz)]
    pltpu.make_async_copy(far, far, top_recv_sem).wait()
    far_rows = []
    for k in range(ops):
        row = jnp.zeros((1, coefs), F32)
        for x in range(k, devices, ops):
            if x >= n_gz:
                row = row + tops[x]
        far_rows.append(row)
    far_columns = jnp.concatenate(far_rows, axis=0).T
    coarse = jnp.zeros((coefs, coefs), F32)
    for k in range(ops):
        coarse = coarse + far_columns[:, k : k + 1] * transfer[k]
    coarse = (32.0 / devices) ** 0.5 * coarse.sum(0, keepdims=True)
    column = jnp.broadcast_to(coarse, (8, coefs)).T[:, 0:1]
    coarse_down = jnp.concatenate(
        [(column * down[k]).sum(0, keepdims=True) for k in range(8)], axis=0
    )
    near = total.reshape(cell_count // 8, 8, coefs)
    local_cells = (near + coarse_down[None]).reshape(cell_count, coefs)
    both = jnp.concatenate(split(local_cells), axis=0)
    for k in range(8):
        staged[:, k, :] = dot3(both, down_high[k], down_low[k])
    out_ref[...] = staged[...].reshape(8 * cell_count, coefs).T

    for copy in cell_copies:
        copy.wait_send()
    pltpu.make_async_copy(far, far, top_send_sem).wait()


def local(sizes, leaf_multipoles, upward_ops, transfer_ops, downward_ops, *lists):
    leaves, coefs = leaf_multipoles.shape
    cell_count = leaves // 8
    ops = transfer_ops.shape[0]
    send_cells, send_count, list_source, list_target, list_count = lists
    n_gz, slots = send_cells.shape[1:]
    devices = sizes[0] * sizes[1] * sizes[2]
    rows = cell_count + n_gz * slots
    vmem = pltpu.VMEM
    weights = lambda n: [vmem((n, coefs, coefs), BF16)] * 2
    operands = (leaf_multipoles.T, upward_ops, transfer_ops, downward_ops, *lists)
    out = pl.pallas_call(
        functools.partial(kernel, sizes),
        out_shape=jax.ShapeDtypeStruct((coefs, leaves), F32),
        in_specs=[pl.BlockSpec(memory_space=pltpu.HBM)] * 9,
        out_specs=pl.BlockSpec(memory_space=pltpu.VMEM),
        scratch_shapes=[
            vmem((coefs, leaves), F32),
            vmem(upward_ops.shape, F32),
            vmem(transfer_ops.shape, F32),
            vmem(downward_ops.shape, F32),
            vmem(send_cells.shape[1:], jnp.int32),
            vmem(send_count.shape, jnp.int32),
            vmem(list_source.shape[1:], jnp.int32),
            vmem(list_target.shape[1:], jnp.int32),
            vmem(list_count.shape, jnp.int32),
            vmem((2 * cell_count, 8 * coefs), BF16),
            *[vmem((ops * coefs, coefs), BF16)] * 2,
            *weights(8),
            vmem((ops * cell_count, rows), BF16),
            vmem((n_gz, slots, coefs), F32),
            vmem((n_gz, slots, coefs), F32),
            vmem((1, coefs), F32),
            vmem((devices, 1, coefs), F32),
            vmem((2 * cell_count, ops * coefs), BF16),
            vmem((cell_count, 8, coefs), F32),
            pltpu.SemaphoreType.DMA((9,)),
            pltpu.SemaphoreType.DMA((n_gz,)),
            pltpu.SemaphoreType.DMA((n_gz,)),
            pltpu.SemaphoreType.DMA,
            pltpu.SemaphoreType.DMA,
        ],
        compiler_params=pltpu.CompilerParams(
            collective_id=0, has_side_effects=True, vmem_limit_bytes=48 << 20
        ),
        cost_estimate=pl.CostEstimate(
            flops=6 * 2 * 32 * cell_count * coefs * coefs,
            bytes_accessed=8_000_000,
            transcendentals=0,
        ),
    )(*(pltpu.with_memory_space_constraint(x, pltpu.HBM) for x in operands))
    return out.T


def solution(mesh):
    sizes = tuple(mesh.shape[name] for name in ("gx", "gy", "gz"))
    split_all = ("gx", "gy", "gz")
    return jax.shard_map(
        functools.partial(local, sizes),
        mesh=mesh,
        in_specs=(
            P(split_all, None),
            P(),
            P(),
            P(),
            P(split_all, None, None),
            P(split_all, None),
            P(split_all, None, None),
            P(split_all, None, None),
            P(split_all, None),
        ),
        out_specs=P(split_all, None),
        check_vma=False,
    )
```

```python
import functools

import jax
import jax.numpy as jnp
from jax import lax
from jax.experimental import pallas as pl
from jax.experimental.pallas import tpu as pltpu
from jax.sharding import PartitionSpec as P

MESH = pl.DeviceIdType.MESH
F32 = jnp.float32
BF16 = jnp.bfloat16
NT = (((1,), (1,)), ((), ()))
TN = (((0,), (0,)), ((), ()))


def split(value):
    high = value.astype(BF16)
    return high, (value - high.astype(F32)).astype(BF16)


def dot(a, b):
    return jnp.dot(a, b, preferred_element_type=F32)


def dot3(both, high, low):
    half = both.shape[0] // 2
    wide = dot(both, high)
    return wide[:half] + wide[half:] + dot(both[:half], low)


def flips(place, size):
    bits = []
    while 1 << len(bits) < size:
        bit = 1 << len(bits)
        bits.append(bit - 2 * bit * lax.rem(lax.div(place, bit), 2))
    return bits


def xor(place, bits, x):
    for i, step in enumerate(bits):
        if isinstance(x, int):
            place = place + step if x >> i & 1 else place
        else:
            place = place + step * lax.rem(lax.div(x, 1 << i), 2)
    return place


def equal(row, length):
    rows = lax.broadcasted_iota(jnp.int32, (length, row.shape[1]), 0)
    return jnp.where(rows == row, 1.0, 0.0).astype(BF16)


def kernel(
    sizes,
    leaf_hbm, up_hbm, transfer_hbm, down_hbm,
    cells_hbm, sends_hbm, source_hbm, target_hbm, counts_hbm,
    out_ref,
    leaf, up, transfer, down,
    cells, sends, source, target, counts,
    leaf_both, transfer_high, transfer_low, down_high, down_low,
    choose, outgoing, received, top_row, tops, picked, staged,
    load_sem, up_sem, send_sem, recv_sem, top_send_sem, top_recv_sem,
):
    n_gx, n_gy, n_gz = sizes
    devices = n_gx * n_gy * n_gz
    coefs, cell_count = leaf.shape[0], leaf.shape[1] // 8
    ops = transfer.shape[0]
    slots = cells.shape[1]
    rows = cell_count + n_gz * slots
    i_gx, i_gy, i_gz = lax.axis_index("gx"), lax.axis_index("gy"), lax.axis_index("gz")

    places = [(i_gx, n_gx, n_gy * n_gz), (i_gy, n_gy, n_gz), (i_gz, n_gz, 1)]
    axes = [(place, flips(place, size), size, below) for place, size, below in places]
    known = [[xor(p, bits, v) for v in range(size)] for p, bits, size, _ in axes]

    def peer(x):
        if isinstance(x, int):
            return tuple(
                table[x // below % size] for table, (_, _, size, below) in zip(known, axes)
            )
        return tuple(
            xor(p, bits, lax.rem(lax.div(x, below), size)) for p, bits, size, below in axes
        )

    def each(low, high, body):
        if devices <= 64:
            for x in range(low, high):
                body(x)
        else:
            lax.fori_loop(low, high, lambda x, c: (body(x), c)[1], 0)

    loads = [
        pltpu.make_async_copy(src, dst, load_sem.at[i])
        for i, (src, dst) in enumerate(
            [
                (leaf_hbm, leaf),
                (up_hbm, up),
                (cells_hbm.at[0], cells),
                (sends_hbm, sends),
                (source_hbm.at[0], source),
                (target_hbm.at[0], target),
                (counts_hbm, counts),
                (transfer_hbm, transfer),
                (down_hbm, down),
            ]
        )
    ]
    up_loads = [
        pltpu.make_async_copy(up_hbm.at[k], up.at[k], up_sem.at[k]) for k in range(8)
    ]
    for load in [loads[0], *up_loads, *loads[2:7]]:
        load.start()

    barrier = pltpu.get_barrier_semaphore()
    each(
        1,
        devices,
        lambda x: pl.semaphore_signal(barrier, inc=1, device_id=peer(x), device_id_type=MESH),
    )

    loads[2].wait()
    loads[3].wait()
    lane = lax.broadcasted_iota(jnp.int32, (1, slots), 1)
    wanted = jnp.concatenate(
        [
            jnp.where(lane < sends[0:1, s : s + 1], cells[s : s + 1, :], -1)
            for s in range(n_gz)
        ],
        axis=1,
    )
    pick = equal(wanted, cell_count)

    loads[0].wait()
    wide = lax.broadcasted_iota(jnp.int32, (256, 256), 1)
    tall = lax.broadcasted_iota(jnp.int32, (256, 256), 0)
    group = jnp.where(wide == tall % 32 * 8 + tall // 32, 1.0, 0.0).astype(BF16)
    for j in range(cell_count // 32):
        for part, first in zip(split(leaf[:, 256 * j : 256 * j + 256]), (0, cell_count)):
            turned = lax.dot_general(group, part, NT, preferred_element_type=F32).astype(BF16)
            for k in range(8):
                leaf_both[
                    first + 32 * j : first + 32 * j + 32, coefs * k : coefs * k + coefs
                ] = turned[32 * k : 32 * k + 32]
    for load in up_loads:
        load.wait()
    loads[7].start()
    loads[8].start()
    cell = dot3(leaf_both[...], *split(up[...].reshape(8 * coefs, coefs)))
    cell_high, cell_low = split(cell)
    out_rows = lax.dot_general(pick, cell_high, TN, preferred_element_type=F32) + lax.dot_general(
        pick, cell_low, TN, preferred_element_type=F32
    )
    outgoing[...] = out_rows.reshape(n_gz, slots, coefs)
    octants = cell.reshape(cell_count // 8, 8, coefs).sum(0).T
    top = jnp.zeros((coefs, coefs), F32)
    for k in range(8):
        top = top + octants[:, k : k + 1] * up[k]
    top_row[...] = (8.0 / cell_count) ** 0.5 * top.sum(0, keepdims=True)
    pl.semaphore_wait(barrier, devices - 1)

    def cell_copy(x):
        to = peer(x)
        return pltpu.make_async_remote_copy(
            src_ref=outgoing.at[to[2]],
            dst_ref=received.at[i_gz],
            send_sem=send_sem.at[x],
            recv_sem=recv_sem.at[x],
            device_id=to,
            device_id_type=MESH,
        )

    cell_copies = [cell_copy(x) for x in range(1, n_gz)]
    for copy in cell_copies:
        copy.start()

    def send_top(x):
        pltpu.make_async_remote_copy(
            src_ref=top_row,
            dst_ref=tops.at[x],
            send_sem=top_send_sem,
            recv_sem=top_recv_sem,
            device_id=peer(x),
            device_id_type=MESH,
        ).start()

    each(n_gz, devices, send_top)

    for load in loads[4:7]:
        load.wait()
    lane = lax.broadcasted_iota(jnp.int32, (1, target.shape[1]), 1)
    for k in range(ops):
        used = jnp.where(lane < counts[0:1, k : k + 1], target[k : k + 1, :], -1)
        choose[pl.ds(k * cell_count, cell_count), :] = lax.dot_general(
            equal(used, cell_count),
            equal(source[k : k + 1, :], rows),
            NT,
            preferred_element_type=F32,
        ).astype(BF16)

    loads[7].wait()
    transfer_high[...], transfer_low[...] = split(transfer[...].reshape(ops * coefs, coefs))
    loads[8].wait()
    for k in range(8):
        down_high[k], down_low[k] = split(down[k])
    received[i_gz] = outgoing[i_gz]

    for copy in cell_copies:
        copy.wait_recv()
    got_high, got_low = split(received[...].reshape(n_gz * slots, coefs))
    table_high = jnp.concatenate([cell_high, got_high], axis=0)
    table_low = jnp.concatenate([cell_low, got_low], axis=0)
    step = 4 * cell_count
    for part, first in ((table_high, 0), (table_low, cell_count)):
        for start in range(0, ops * cell_count, step):
            rows_picked = dot(choose[start : start + step, :], part).astype(BF16)
            for k in range(4):
                lane = coefs * (start // cell_count + k)
                picked[first : first + cell_count, lane : lane + coefs] = rows_picked[
                    cell_count * k : cell_count * k + cell_count
                ]
    total = dot3(picked[...], transfer_high[...], transfer_low[...])

    far = tops.at[pl.ds(n_gz, devices - n_gz)]
    pltpu.make_async_copy(far, far, top_recv_sem).wait()
    far_rows = []
    for k in range(ops):
        row = jnp.zeros((1, coefs), F32)
        for x in range(k, devices, ops):
            if x >= n_gz:
                row = row + tops[x]
        far_rows.append(row)
    far_columns = jnp.concatenate(far_rows, axis=0).T
    coarse = jnp.zeros((coefs, coefs), F32)
    for k in range(ops):
        coarse = coarse + far_columns[:, k : k + 1] * transfer[k]
    coarse = (32.0 / devices) ** 0.5 * coarse.sum(0, keepdims=True)
    column = jnp.broadcast_to(coarse, (8, coefs)).T[:, 0:1]
    coarse_down = jnp.concatenate(
        [(column * down[k]).sum(0, keepdims=True) for k in range(8)], axis=0
    )
    near = total.reshape(cell_count // 8, 8, coefs)
    local_cells = (near + coarse_down[None]).reshape(cell_count, coefs)
    both = jnp.concatenate(split(local_cells), axis=0)
    for k in range(8):
        staged[:, k, :] = dot3(both, down_high[k], down_low[k])
    same = equal(lax.broadcasted_iota(jnp.int32, (1, coefs), 1), coefs)
    for j in range(cell_count // 32):
        high, low = split(staged[32 * j : 32 * j + 32].reshape(256, coefs))
        out_ref[:, 256 * j : 256 * j + 256] = lax.dot_general(
            same, high, NT, preferred_element_type=F32
        ) + lax.dot_general(same, low, NT, preferred_element_type=F32)

    for copy in cell_copies:
        copy.wait_send()
    pltpu.make_async_copy(far, far, top_send_sem).wait()


def local(sizes, leaf_multipoles, upward_ops, transfer_ops, downward_ops, *lists):
    leaves, coefs = leaf_multipoles.shape
    cell_count = leaves // 8
    ops = transfer_ops.shape[0]
    send_cells, send_count, list_source, list_target, list_count = lists
    n_gz, slots = send_cells.shape[1:]
    devices = sizes[0] * sizes[1] * sizes[2]
    rows = cell_count + n_gz * slots
    vmem = pltpu.VMEM
    weights = lambda n: [vmem((n, coefs, coefs), BF16)] * 2
    operands = (leaf_multipoles.T, upward_ops, transfer_ops, downward_ops, *lists)
    out = pl.pallas_call(
        functools.partial(kernel, sizes),
        out_shape=jax.ShapeDtypeStruct((coefs, leaves), F32),
        in_specs=[pl.BlockSpec(memory_space=pltpu.HBM)] * 9,
        out_specs=pl.BlockSpec(memory_space=pltpu.VMEM),
        scratch_shapes=[
            vmem((coefs, leaves), F32),
            vmem(upward_ops.shape, F32),
            vmem(transfer_ops.shape, F32),
            vmem(downward_ops.shape, F32),
            vmem(send_cells.shape[1:], jnp.int32),
            vmem(send_count.shape, jnp.int32),
            vmem(list_source.shape[1:], jnp.int32),
            vmem(list_target.shape[1:], jnp.int32),
            vmem(list_count.shape, jnp.int32),
            vmem((2 * cell_count, 8 * coefs), BF16),
            *[vmem((ops * coefs, coefs), BF16)] * 2,
            *weights(8),
            vmem((ops * cell_count, rows), BF16),
            vmem((n_gz, slots, coefs), F32),
            vmem((n_gz, slots, coefs), F32),
            vmem((1, coefs), F32),
            vmem((devices, 1, coefs), F32),
            vmem((2 * cell_count, ops * coefs), BF16),
            vmem((cell_count, 8, coefs), F32),
            pltpu.SemaphoreType.DMA((9,)),
            pltpu.SemaphoreType.DMA((8,)),
            pltpu.SemaphoreType.DMA((n_gz,)),
            pltpu.SemaphoreType.DMA((n_gz,)),
            pltpu.SemaphoreType.DMA,
            pltpu.SemaphoreType.DMA,
        ],
        compiler_params=pltpu.CompilerParams(
            collective_id=0, has_side_effects=True, vmem_limit_bytes=48 << 20
        ),
        cost_estimate=pl.CostEstimate(
            flops=6 * 2 * 32 * cell_count * coefs * coefs,
            bytes_accessed=8_000_000,
            transcendentals=0,
        ),
    )(*(pltpu.with_memory_space_constraint(x, pltpu.HBM) for x in operands))
    return out.T


def solution(mesh):
    sizes = tuple(mesh.shape[name] for name in ("gx", "gy", "gz"))
    split_all = ("gx", "gy", "gz")
    return jax.shard_map(
        functools.partial(local, sizes),
        mesh=mesh,
        in_specs=(
            P(split_all, None),
            P(),
            P(),
            P(),
            P(split_all, None, None),
            P(split_all, None),
            P(split_all, None, None),
            P(split_all, None, None),
            P(split_all, None),
        ),
        out_specs=P(split_all, None),
        check_vma=False,
    )
```
